32 devices in a mesh: dp: 4 (over z), gx: 2 (over y), gy: 4 (over x, core).
Axes of the slice: x: 2, y: 2, z: 4, core: 2. Of those that a mesh axis runs over, the one named last changes fastest.
Arguments:
- volume: bfloat16 [4, 64, 96, 4, 128], P('dp', 'gx', 'gy'), may hold values from -6 to 6
- cotangent: bfloat16 [4, 32, 48, 2, 128], P('dp', 'gx', 'gy'), may hold values from -6 to 6
- w_first: bfloat16 [27, 128, 128], replicated, may hold values from -0.109375 to 0.109375
- w_second: bfloat16 [27, 128, 128], replicated, may hold values from -0.109375 to 0.109375
Outputs:
- grad_volume: bfloat16 [4, 64, 96, 4, 128], P('dp', 'gx', 'gy')
- grad_first: float32 [27, 128, 128], P(None, ('gx', 'gy'))
- grad_second: float32 [27, 128, 128], P(None, ('gx', 'gy'))
The draws below stay inside these ranges and needn't reach their ends.
All inputs are finite; a program needn't handle non-finite values.
Results may differ from the reference program's by a relative error of at most 0.0095.
Values may be sent and summed in bfloat16 or wider, within the bound.
A program may use at most 64 MiB of HBM per device.

```python
import jax
import jax.numpy as jnp
from jax import lax

C = 128
ZC = 4
TOMOS = 4
NX = 64
NY = 96


def steps_of(stream_key, shape, shards, low, largest):
    def one(position, parts):
        draws = jax.random.uniform(jax.random.fold_in(jax.random.fold_in(stream_key, 6), position), (parts,), jnp.float32, low / len(shards), largest / len(shards))
        return jnp.repeat(jnp.exp(draws), shape[position] // parts).reshape((-1,) + (1,) * (len(shape) - position - 1))

    gain = one(*shards[0])
    for cut in shards[1:]:
        gain = gain * one(*cut)
    return gain


def centred(key, extent, width, limit, shards=(), dtype=jnp.bfloat16):
    drawn = jax.random.normal(key, extent, jnp.float32) * width
    if len(shards) > 0:
        drawn = steps_of(key, extent, shards, -0.22, 0.18) * drawn
    return jnp.clip(drawn, min=-limit, max=limit).astype(dtype)


def setup_inputs(seed: int = 0) -> dict:
    key_of = jax.random.split(jax.random.key(seed), 5)
    return {
        "volume": centred(key_of[0], (TOMOS, NX, NY, ZC, C), 1.0, 6.0, ((0, 4), (1, 2), (2, 4))),
        "cotangent": centred(key_of[1], (TOMOS, NX // 2, NY // 2, ZC // 2, C), 1.0, 6.0, ((0, 4), (1, 2), (2, 4))),
        "w_first": centred(key_of[2], (27, C, C), (27 * C) ** -0.5, 0.109375),
        "w_second": centred(key_of[3], (27, C, C), (27 * C) ** -0.5, 0.109375),
    }


def convolve(values, weights, stride):
    channels = weights.shape[1]
    kernel = weights.reshape(3, 3, 3, channels, channels)
    return lax.conv_general_dilated(values, kernel, (stride, stride, stride), ((1, 1), (1, 1), (1, 1)), dimension_numbers=('NDHWC', 'DHWIO', 'NDHWC'), precision=lax.Precision.HIGHEST, preferred_element_type=jnp.float32)

def reference(volume, cotangent, w_first, w_second):
    volume_full = volume.astype(jnp.float32)
    first_full = w_first.astype(jnp.float32)
    second_full = w_second.astype(jnp.float32)
    preact, first_back = jax.vjp(lambda values, weights: convolve(values, weights, 1), volume_full, first_full)
    hidden = jax.nn.silu(preact).astype(jnp.bfloat16)
    hidden_full = hidden.astype(jnp.float32)
    strided, second_back = jax.vjp(lambda values, weights: convolve(values, weights, 2), hidden_full, second_full)
    grad_hidden, grad_second = second_back(cotangent.astype(jnp.float32))
    sigma = jax.nn.sigmoid(preact)
    grad_pre = (grad_hidden * sigma * (1.0 + preact * (1.0 - sigma))).astype(jnp.bfloat16)
    grad_volume, grad_first = first_back(grad_pre.astype(jnp.float32))
    return (grad_volume.astype(jnp.bfloat16), grad_first, grad_second)
```

```python
import jax
import jax.numpy as jnp
from jax import lax
from jax.experimental import pallas as pl
from jax.experimental.pallas import tpu as pltpu
from jax.sharding import PartitionSpec as P

BF = jnp.bfloat16
F32 = jnp.float32
NT = (((1,), (1,)), ((), ()))
PAIRS = (((1, 0),), ((0, 1), (2, 0)))


def wide(cells):
    gx, gy = lax.axis_size("gx"), lax.axis_size("gy")
    up = lambda a, n, v: lax.ppermute(v, a, [(i, i + 1) for i in range(n - 1)])
    down = lambda a, n, v: lax.ppermute(v, a, [(i + 1, i) for i in range(n - 1)])
    cells = jnp.concatenate([up("gy", gy, cells[:, -1:]), cells, down("gy", gy, cells[:, :1])], 1)
    even, odd = cells[0], cells[1]
    before = jnp.concatenate([up("gx", gx, odd[:, -1:]), odd[:, :-1]], 1)
    after = jnp.concatenate([even[:, 1:], down("gx", gx, even[:, :1])], 1)
    return jnp.stack([before, even, odd, after])


def coarse(cells):
    gx, gy = lax.axis_size("gx"), lax.axis_size("gy")
    down = lambda a, n, v: lax.ppermute(v, a, [(i + 1, i) for i in range(n - 1)])
    cells = jnp.concatenate([cells, down("gy", gy, cells[:1])], 0)
    following = jnp.concatenate([cells[:, 1:], down("gx", gx, cells[:, :1])], 1)
    return jnp.stack([cells, following])


def conv_dot(x_ref, w_ref, bands, px, half, transposed):
    ny, nm = x_ref.shape[1] - 2, x_ref.shape[2]
    c = w_ref.shape[1]
    lo = half * c
    parts = [
        x_ref[px + a, b : b + ny, :, lo : lo + 3 * c].reshape(ny * nm, 3 * c)
        for a in range(3)
        for b in range(3)
    ]
    lhs = jnp.concatenate(parts, 1)
    if transposed:
        return lax.dot_general(lhs, bands[half], NT, preferred_element_type=F32)
    return jnp.dot(lhs, bands[half], preferred_element_type=F32)


def fill_bands(w_ref, bands, transposed):
    c = w_ref.shape[1]
    zero = jnp.zeros((c, c), BF)
    for half in range(2):
        for s in range(9):
            for k in range(3):
                for o in range(2):
                    tap = (k + half) - (o + 2 * half) + 1
                    good = 0 <= tap <= 2
                    rows = slice((3 * s + k) * c, (3 * s + k + 1) * c)
                    cols = slice(o * c, (o + 1) * c)
                    if transposed:
                        bands[half, cols, rows] = w_ref[26 - 3 * s - tap] if good else zero
                    else:
                        bands[half, rows, cols] = w_ref[3 * s + tap] if good else zero


def grads_kernel(x_ref, c_ref, w1_ref, w2_ref, gp_ref, g1_ref, g2_ref, bands, pre, gh, hid_t, gp_t, hid):
    ny, nm = x_ref.shape[1] - 2, x_ref.shape[2]
    nj = ny // 2
    c = w1_ref.shape[1]
    fill_bands(w1_ref, bands, False)
    for px in range(2):
        for half in range(2):
            pre[px, :, 2 * half * c : 2 * (half + 1) * c] = conv_dot(x_ref, w1_ref, bands, px, half, False)
    zero = jnp.zeros((c, c), BF)
    for px in range(2):
        for py in range(2):
            total = None
            for a, ci in PAIRS[px]:
                for b, dj in PAIRS[py]:
                    w = lambda t: w2_ref[9 * a + 3 * b + t]
                    left = jnp.concatenate([w(1), w(2), zero, zero], 0)
                    right = jnp.concatenate([zero, w(0), w(1), w(2)], 0)
                    rhs = jnp.concatenate([left, right], 1)
                    lhs = c_ref[ci, dj : dj + nj].reshape(nj * nm, 2 * c)
                    term = lax.dot_general(lhs, rhs, NT, preferred_element_type=F32)
                    total = term if total is None else total + term
            gh[px, :, py] = total.reshape(nj, nm, 4 * c)

    for px in range(2):
        def cells(j, _):
            for py in range(2):
                y = 2 * j + py
                v = pre[px, pl.ds(pl.multiple_of(y * nm, nm), nm), :]
                sigma = jax.nn.sigmoid(v)
                hid[px, py, j] = (v * sigma).astype(BF)
                gp_ref[px, y] = (gh[px, j, py] * (sigma * (1.0 + v * (1.0 - sigma)))).astype(BF)
            return _

        lax.fori_loop(0, nj, cells, 0)
    for px in range(2):
        gp_t[:, px * ny * nm : (px + 1) * ny * nm] = gp_ref[px].reshape(ny * nm, 4 * c).T
        for py in range(2):
            hid_t[px, py] = hid[px, py].reshape(nj * nm, 4 * c).T
    for a in range(3):
        px = 0 if a == 1 else 1
        ci = 1 if a == 0 else 0
        for b in range(3):
            py = 0 if b == 1 else 1
            dj = 1 if b == 0 else 0
            rhs = c_ref[ci, dj : dj + nj].reshape(nj * nm, 2 * c)
            r = jnp.dot(hid_t[px, py], rhs, preferred_element_type=F32)
            blk = lambda z, k: r[z * c : (z + 1) * c, k * c : (k + 1) * c]
            t = 9 * a + 3 * b
            g2_ref[t] = blk(1, 1).astype(BF)
            g2_ref[t + 1] = (blk(0, 0) + blk(2, 1)).astype(BF)
            g2_ref[t + 2] = (blk(1, 0) + blk(3, 1)).astype(BF)
    for a in range(3):
        for b in range(3):
            sums = [None, None, None]
            for half in range(2):
                rhs = jnp.concatenate(
                    [
                        x_ref[px + a, b : b + ny, :, half * c : (half + 3) * c].reshape(ny * nm, 3 * c)
                        for px in range(2)
                    ],
                    0,
                )
                r = jnp.dot(gp_t[2 * half * c : 2 * (half + 1) * c, :], rhs, preferred_element_type=F32)
                for o in range(2):
                    for k in range(3):
                        tap = (k + half) - (o + 2 * half) + 1
                        if 0 <= tap <= 2:
                            term = r[o * c : (o + 1) * c, k * c : (k + 1) * c]
                            sums[tap] = term if sums[tap] is None else sums[tap] + term
            for tap in range(3):
                g1_ref[9 * a + 3 * b + tap] = sums[tap].T.astype(BF)


def volume_kernel(x_ref, w_ref, out_ref, bands):
    ny, nm = x_ref.shape[1] - 2, x_ref.shape[2]
    c = w_ref.shape[1]
    fill_bands(w_ref, bands, True)
    for px in range(2):
        for half in range(2):
            r = conv_dot(x_ref, w_ref, bands, px, half, True)
            out_ref[px, :, :, 2 * half * c : 2 * (half + 1) * c] = r.reshape(ny, nm, 2 * c).astype(BF)


VMEM = pl.BlockSpec(memory_space=pltpu.VMEM)
PARAMS = pltpu.CompilerParams(vmem_limit_bytes=48 * 1024 * 1024)


def local(volume, cotangent, w_first, w_second):
    _, nx, ny, nz, c = volume.shape
    nm, nj, lanes = nx // 2, ny // 2, nz * c
    split = volume.reshape(nm, 2, ny, lanes).transpose(1, 2, 0, 3)
    cells = wide(split)
    grads = coarse(cotangent.reshape(nm, nj, 2 * c).transpose(1, 0, 2))
    weight = jax.ShapeDtypeStruct((27, c, c), BF)
    grad_pre, first, second = pl.pallas_call(
        grads_kernel,
        out_shape=(jax.ShapeDtypeStruct((2, ny, nm, lanes), BF), weight, weight),
        in_specs=[VMEM] * 4,
        out_specs=(VMEM,) * 3,
        scratch_shapes=[
            pltpu.VMEM((2, 27 * c, 2 * c), BF),
            pltpu.VMEM((2, ny * nm, lanes), F32),
            pltpu.VMEM((2, nj, 2, nm, lanes), F32),
            pltpu.VMEM((2, 2, lanes, nj * nm), BF),
            pltpu.VMEM((lanes, 2 * ny * nm), BF),
            pltpu.VMEM((2, 2, nj, nm, lanes), BF),
        ],
        compiler_params=PARAMS,
    )(cells, grads, w_first, w_second)
    both = jnp.stack([first, second])
    share = lax.psum_scatter(both, ("gx", "gy"), scatter_dimension=2, tiled=True)
    share = lax.psum(share, "dp").astype(F32)
    out = pl.pallas_call(
        volume_kernel,
        out_shape=jax.ShapeDtypeStruct((2, ny, nm, lanes), BF),
        in_specs=[VMEM] * 2,
        out_specs=VMEM,
        scratch_shapes=[pltpu.VMEM((2, 2 * c, 27 * c), BF)],
        compiler_params=PARAMS,
    )(wide(grad_pre), w_first)
    grad_volume = out.transpose(2, 0, 1, 3).reshape(1, nx, ny, nz, c)
    return (grad_volume, share[0], share[1])


def solution(mesh):
    return jax.shard_map(
        local,
        mesh=mesh,
        in_specs=(P("dp", "gx", "gy", None, None), P("dp", "gx", "gy", None, None), P(), P()),
        out_specs=(
            P("dp", "gx", "gy", None, None),
            P(None, ("gx", "gy"), None),
            P(None, ("gx", "gy"), None),
        ),
        check_vma=False,
    )
```

```python
import functools

import jax
import jax.numpy as jnp
from jax import lax
from jax.experimental import pallas as pl
from jax.experimental.pallas import tpu as pltpu
from jax.sharding import PartitionSpec as P

BF = jnp.bfloat16
F32 = jnp.float32
NT = (((1,), (1,)), ((), ()))
PAIRS = (((1, 0),), ((0, 1), (2, 0)))


def wide(cells):
    gx, gy = lax.axis_size("gx"), lax.axis_size("gy")
    up = lambda a, n, v: lax.ppermute(v, a, [(i, i + 1) for i in range(n - 1)])
    down = lambda a, n, v: lax.ppermute(v, a, [(i + 1, i) for i in range(n - 1)])
    cells = jnp.concatenate([up("gy", gy, cells[:, -1:]), cells, down("gy", gy, cells[:, :1])], 1)
    even, odd = cells[0], cells[1]
    before = jnp.concatenate([up("gx", gx, odd[:, -1:]), odd[:, :-1]], 1)
    after = jnp.concatenate([even[:, 1:], down("gx", gx, even[:, :1])], 1)
    return jnp.stack([before, even, odd, after])


def coarse(cells):
    gx, gy = lax.axis_size("gx"), lax.axis_size("gy")
    down = lambda a, n, v: lax.ppermute(v, a, [(i + 1, i) for i in range(n - 1)])
    cells = jnp.concatenate([cells, down("gy", gy, cells[:1])], 0)
    following = jnp.concatenate([cells[:, 1:], down("gx", gx, cells[:, :1])], 1)
    return jnp.stack([cells, following])


def conv_dot(x_ref, w_ref, bands, px, half, transposed):
    ny, nm = x_ref.shape[1] - 2, x_ref.shape[2]
    c = w_ref.shape[1]
    lo = half * c
    parts = [
        x_ref[px + a, b : b + ny, :, lo : lo + 3 * c].reshape(ny * nm, 3 * c)
        for a in range(3)
        for b in range(3)
    ]
    lhs = jnp.concatenate(parts, 1)
    if transposed:
        return lax.dot_general(lhs, bands[half], NT, preferred_element_type=F32)
    return jnp.dot(lhs, bands[half], preferred_element_type=F32)


def fill_bands(w_ref, bands, transposed):
    c = w_ref.shape[1]
    zero = jnp.zeros((c, c), BF)
    for half in range(2):
        for s in range(9):
            for k in range(3):
                for o in range(2):
                    tap = (k + half) - (o + 2 * half) + 1
                    good = 0 <= tap <= 2
                    rows = slice((3 * s + k) * c, (3 * s + k + 1) * c)
                    cols = slice(o * c, (o + 1) * c)
                    if transposed:
                        bands[half, cols, rows] = w_ref[26 - 3 * s - tap] if good else zero
                    else:
                        bands[half, rows, cols] = w_ref[3 * s + tap] if good else zero


def grads_kernel(x_ref, c_ref, w1_ref, w2_ref, gp_ref, g1_ref, g2_ref, bands, pre, gh, hid_t, gp_t, hid):
    ny, nm = x_ref.shape[1] - 2, x_ref.shape[2]
    nj = ny // 2
    c = w1_ref.shape[1]
    fill_bands(w1_ref, bands, False)
    for px in range(2):
        for half in range(2):
            pre[px, :, 2 * half * c : 2 * (half + 1) * c] = conv_dot(x_ref, w1_ref, bands, px, half, False)
    zero = jnp.zeros((c, c), BF)
    for px in range(2):
        for py in range(2):
            total = None
            for a, ci in PAIRS[px]:
                for b, dj in PAIRS[py]:
                    w = lambda t: w2_ref[9 * a + 3 * b + t]
                    left = jnp.concatenate([w(1), w(2), zero, zero], 0)
                    right = jnp.concatenate([zero, w(0), w(1), w(2)], 0)
                    rhs = jnp.concatenate([left, right], 1)
                    lhs = c_ref[ci, dj : dj + nj].reshape(nj * nm, 2 * c)
                    term = lax.dot_general(lhs, rhs, NT, preferred_element_type=F32)
                    total = term if total is None else total + term
            gh[px, :, py] = total.reshape(nj, nm, 4 * c)

    for px in range(2):
        def cells(j, _):
            for py in range(2):
                y = 2 * j + py
                v = pre[px, pl.ds(pl.multiple_of(y * nm, nm), nm), :]
                sigma = jax.nn.sigmoid(v)
                hid[px, py, j] = (v * sigma).astype(BF)
                gp_ref[px, y] = (gh[px, j, py] * (sigma * (1.0 + v * (1.0 - sigma)))).astype(BF)
            return _

        lax.fori_loop(0, nj, cells, 0)
    for px in range(2):
        gp_t[:, px * ny * nm : (px + 1) * ny * nm] = gp_ref[px].reshape(ny * nm, 4 * c).T
        for py in range(2):
            hid_t[px, py] = hid[px, py].reshape(nj * nm, 4 * c).T
    for a in range(3):
        px = 0 if a == 1 else 1
        ci = 1 if a == 0 else 0
        for b in range(3):
            py = 0 if b == 1 else 1
            dj = 1 if b == 0 else 0
            rhs = c_ref[ci, dj : dj + nj].reshape(nj * nm, 2 * c)
            r = jnp.dot(hid_t[px, py], rhs, preferred_element_type=F32)
            blk = lambda z, k: r[z * c : (z + 1) * c, k * c : (k + 1) * c]
            t = 9 * a + 3 * b
            g2_ref[t] = blk(1, 1).astype(BF)
            g2_ref[t + 1] = (blk(0, 0) + blk(2, 1)).astype(BF)
            g2_ref[t + 2] = (blk(1, 0) + blk(3, 1)).astype(BF)
    for a in range(3):
        for b in range(3):
            sums = [None, None, None]
            for half in range(2):
                rhs = jnp.concatenate(
                    [
                        x_ref[px + a, b : b + ny, :, half * c : (half + 3) * c].reshape(ny * nm, 3 * c)
                        for px in range(2)
                    ],
                    0,
                )
                r = jnp.dot(gp_t[2 * half * c : 2 * (half + 1) * c, :], rhs, preferred_element_type=F32)
                for o in range(2):
                    for k in range(3):
                        tap = (k + half) - (o + 2 * half) + 1
                        if 0 <= tap <= 2:
                            term = r[o * c : (o + 1) * c, k * c : (k + 1) * c]
                            sums[tap] = term if sums[tap] is None else sums[tap] + term
            for tap in range(3):
                g1_ref[9 * a + 3 * b + tap] = sums[tap].T.astype(BF)


def volume_kernel(x_ref, w_ref, out_ref, bands):
    ny, nm = x_ref.shape[1] - 2, x_ref.shape[2]
    c = w_ref.shape[1]
    fill_bands(w_ref, bands, True)
    for px in range(2):
        for half in range(2):
            r = conv_dot(x_ref, w_ref, bands, px, half, True)
            out_ref[px, :, :, 2 * half * c : 2 * (half + 1) * c] = r.reshape(ny, nm, 2 * c).astype(BF)


VMEM = pl.BlockSpec(memory_space=pltpu.VMEM)
PARAMS = pltpu.CompilerParams(vmem_limit_bytes=48 * 1024 * 1024)


def plane_orders(gx, gy):
    gys = [("gy", 1 << k) for k in range(gy.bit_length() - 1)]
    gxs = [("gx", 1 << k) for k in range(gx.bit_length() - 1)]
    return (gys + gxs, gys[:1] + gxs + gys[1:])


def by_halves(grad, order, gx, gy):
    taps, c, _ = grad.shape
    bits = [("gx", 1 << k) for k in reversed(range(gx.bit_length() - 1))]
    bits += [("gy", 1 << k) for k in reversed(range(gy.bit_length() - 1))]
    share = c // (gx * gy)
    parts = grad.reshape((taps,) + (2,) * len(bits) + (share, c))
    n = len(bits)
    parts = parts.transpose(tuple(1 + bits.index(o) for o in order) + (0, n + 1, n + 2))
    return parts.reshape(gx * gy, taps * share, c)


def reduce_kernel(orders, dps, first_ref, second_ref, out1_ref, out2_ref, *scratch):
    steps = len(orders[0]) + len(dps)
    lands, sums = scratch[:steps], scratch[steps : 2 * steps - 1]
    send_sem, recv_sem = scratch[-2:]
    outs = (out1_ref, out2_ref)

    def side(axis, bit):
        at = lax.axis_index(axis)
        mine = (at // bit) % 2
        return mine, {axis: at + bit * (1 - 2 * mine)}

    barrier = pltpu.get_barrier_semaphore()
    for axis, bit in orders[0] + dps:
        pl.semaphore_signal(
            barrier, inc=1, device_id=side(axis, bit)[1], device_id_type=pl.DeviceIdType.MESH
        )
    pl.semaphore_wait(barrier, steps)

    held = [first_ref, second_ref]
    halving = len(orders[0])
    plans = [orders[0] + dps, orders[1] + dps[::-1]]
    for k in range(steps):
        copies = []
        for s in range(2):
            mine, partner = side(*plans[s][k])
            size = lands[k].shape[1]
            src = held[s].at[pl.ds((1 - mine) * size, size)] if k < halving else held[s]
            copy = pltpu.make_async_remote_copy(
                src_ref=src,
                dst_ref=lands[k].at[s],
                send_sem=send_sem.at[k, s],
                recv_sem=recv_sem.at[k, s],
                device_id=partner,
                device_id_type=pl.DeviceIdType.MESH,
            )
            copy.start()
            copies.append(copy)
        following = []
        for s in range(2):
            copies[s].wait()
            mine, _ = side(*plans[s][k])
            size = lands[k].shape[1]
            target = outs[s] if k == steps - 1 else sums[k].at[s]
            base = mine * size if k < halving else 0

            def add(i, _):
                total = held[s][base + i].astype(F32) + lands[k][s, i].astype(F32)
                target[i] = total.astype(target.dtype)
                return _

            lax.fori_loop(0, size, add, 0)
            following.append(target)
        held = following


def reduce_grads(first, second):
    gx, gy, dp = (lax.axis_size(a) for a in ("gx", "gy", "dp"))
    orders = plane_orders(gx, gy)
    dps = [("dp", 1 << k) for k in range(dp.bit_length() - 1)]
    taps, c, _ = first.shape
    share = c // (gx * gy)
    rows = taps * share
    sizes = [gx * gy >> (k + 1) for k in range(len(orders[0]))] + [1] * len(dps)
    out = jax.ShapeDtypeStruct((1, rows, c), F32)
    one, two = pl.pallas_call(
        functools.partial(reduce_kernel, orders, dps),
        out_shape=(out, out),
        in_specs=[VMEM] * 2,
        out_specs=(VMEM,) * 2,
        scratch_shapes=[pltpu.VMEM((2, n, rows, c), BF) for n in sizes]
        + [pltpu.VMEM((2, n, rows, c), BF) for n in sizes[:-1]]
        + [pltpu.SemaphoreType.DMA((len(sizes), 2)), pltpu.SemaphoreType.DMA((len(sizes), 2))],
        compiler_params=pltpu.CompilerParams(
            collective_id=0, has_side_effects=True, vmem_limit_bytes=48 * 1024 * 1024
        ),
    )(by_halves(first, orders[0], gx, gy), by_halves(second, orders[1], gx, gy))
    return one.reshape(taps, share, c), two.reshape(taps, share, c)


def local(volume, cotangent, w_first, w_second):
    _, nx, ny, nz, c = volume.shape
    nm, nj, lanes = nx // 2, ny // 2, nz * c
    split = volume.reshape(nm, 2, ny, lanes).transpose(1, 2, 0, 3)
    cells = wide(split)
    grads = coarse(cotangent.reshape(nm, nj, 2 * c).transpose(1, 0, 2))
    weight = jax.ShapeDtypeStruct((27, c, c), BF)
    grad_pre, first, second = pl.pallas_call(
        grads_kernel,
        out_shape=(jax.ShapeDtypeStruct((2, ny, nm, lanes), BF), weight, weight),
        in_specs=[VMEM] * 4,
        out_specs=(VMEM,) * 3,
        scratch_shapes=[
            pltpu.VMEM((2, 27 * c, 2 * c), BF),
            pltpu.VMEM((2, ny * nm, lanes), F32),
            pltpu.VMEM((2, nj, 2, nm, lanes), F32),
            pltpu.VMEM((2, 2, lanes, nj * nm), BF),
            pltpu.VMEM((lanes, 2 * ny * nm), BF),
            pltpu.VMEM((2, 2, nj, nm, lanes), BF),
        ],
        compiler_params=PARAMS,
    )(cells, grads, w_first, w_second)
    share = reduce_grads(first, second)
    out = pl.pallas_call(
        volume_kernel,
        out_shape=jax.ShapeDtypeStruct((2, ny, nm, lanes), BF),
        in_specs=[VMEM] * 2,
        out_specs=VMEM,
        scratch_shapes=[pltpu.VMEM((2, 2 * c, 27 * c), BF)],
        compiler_params=PARAMS,
    )(wide(grad_pre), w_first)
    grad_volume = out.transpose(2, 0, 1, 3).reshape(1, nx, ny, nz, c)
    return (grad_volume, share[0], share[1])


def solution(mesh):
    return jax.shard_map(
        local,
        mesh=mesh,
        in_specs=(P("dp", "gx", "gy", None, None), P("dp", "gx", "gy", None, None), P(), P()),
        out_specs=(
            P("dp", "gx", "gy", None, None),
            P(None, ("gx", "gy"), None),
            P(None, ("gx", "gy"), None),
        ),
        check_vma=False,
    )
```

```python
import functools

import jax
import jax.numpy as jnp
from jax import lax
from jax.experimental import pallas as pl
from jax.experimental.pallas import tpu as pltpu
from jax.sharding import PartitionSpec as P

BF = jnp.bfloat16
F32 = jnp.float32
VMEM = pl.BlockSpec(memory_space=pltpu.VMEM)
NT = (((1,), (1,)), ((), ()))
PAIRS = (((1, 0),), ((0, 1), (2, 0)))


TURNS = [(dx, dy) for dx in (1, -1, 0) for dy in (1, -1, 0)][:8]


def swap_kernel(ys_ref, xs_ref, land_ref, send_sem, recv_sem):
    gx, gy = lax.axis_size("gx"), lax.axis_size("gy")
    x, y = lax.axis_index("gx"), lax.axis_index("gy")
    partners = [{"gx": (x + dx + gx) % gx, "gy": (y + dy + gy) % gy} for dx, dy in TURNS]
    barrier = pltpu.get_barrier_semaphore()
    for partner in partners:
        pl.semaphore_signal(barrier, inc=1, device_id=partner, device_id_type=pl.DeviceIdType.MESH)
    pl.semaphore_wait(barrier, len(TURNS))
    copies = []
    for k, (dx, dy) in enumerate(TURNS):
        src = ys_ref.at[(1 + dy) // 2] if dx == 0 else xs_ref.at[(1 + dx) // 2]
        copy = pltpu.make_async_remote_copy(
            src_ref=src,
            dst_ref=land_ref.at[k],
            send_sem=send_sem.at[k],
            recv_sem=recv_sem.at[k],
            device_id=partners[k],
            device_id_type=pl.DeviceIdType.MESH,
        )
        copy.start()
        copies.append(copy)
    for copy in copies:
        copy.wait()


def swap(ys, xs, place):
    land = pl.pallas_call(
        swap_kernel,
        out_shape=jax.ShapeDtypeStruct((8,) + ys.shape[1:], BF),
        in_specs=[VMEM] * 2,
        out_specs=VMEM,
        scratch_shapes=[pltpu.SemaphoreType.DMA((8,)), pltpu.SemaphoreType.DMA((8,))],
        compiler_params=pltpu.CompilerParams(collective_id=place, has_side_effects=True),
    )(ys, xs)
    out = {}
    x, y = lax.axis_index("gx"), lax.axis_index("gy")
    has_x = {0: True, 1: x > 0, -1: x < lax.axis_size("gx") - 1}
    has_y = {0: True, 1: y > 0, -1: y < lax.axis_size("gy") - 1}
    for k, (dx, dy) in enumerate(TURNS):
        good = jnp.logical_and(has_x[dx], has_y[dy])
        out[dx, dy] = jnp.where(good, land[k], jnp.zeros((), BF))
    return out


def padded(rows, count, lanes):
    return jnp.pad(rows, ((0, count - rows.shape[0]), (0, lanes - rows.shape[1])))


def edges(cells):
    _, ny, nm, lanes = cells.shape
    rows = -(-max(2 * nm, ny) // 16) * 16
    ys = [padded(cells[:, y].reshape(2 * nm, lanes), rows, lanes) for y in (0, ny - 1)]
    xs = [padded(row, rows, lanes) for row in (cells[0, :, 0], cells[1, :, nm - 1])]
    return ys, xs


def widened(cells, got):
    _, ny, nm, lanes = cells.shape
    layer = lambda dy: got[0, dy][: 2 * nm].reshape(2, 1, nm, lanes)
    cells = jnp.concatenate([layer(1), cells, layer(-1)], 1)

    def column(dx):
        parts = [got[dx, 1][ny - 1 : ny], got[dx, 0][:ny], got[dx, -1][:1]]
        return jnp.concatenate(parts, 0)[:, None]

    even, odd = cells[0], cells[1]
    before = jnp.concatenate([column(1), odd[:, :-1]], 1)
    after = jnp.concatenate([even[:, 1:], column(-1)], 1)
    return jnp.stack([before, even, odd, after])


def widened_both(cells, coarse):
    lanes = cells.shape[3]
    nj, ni, few = coarse.shape
    ys, xs = edges(cells)
    top = ys[0].shape[0]
    more = -(-max(nj, ni) // 16) * 16
    low = lambda rows: padded(rows, more, lanes)
    blank = jnp.zeros((more, lanes), BF)
    ys = jnp.stack([jnp.concatenate([ys[0], low(coarse[0])]), jnp.concatenate([ys[1], blank])])
    xs = jnp.stack([jnp.concatenate([xs[0], low(coarse[:, 0])]), jnp.concatenate([xs[1], blank])])
    got = swap(ys, xs, 1)
    tail = lambda dx, dy, n: got[dx, dy][top : top + n, :few]
    long = jnp.concatenate([coarse, tail(0, -1, ni)[None]], 0)
    column = jnp.concatenate([tail(-1, 0, nj), tail(-1, -1, 1)], 0)[:, None]
    following = jnp.concatenate([long[:, 1:], column], 1)
    return widened(cells, got), jnp.stack([long, following])


def widened_again(cells):
    ys, xs = edges(cells)
    return widened(cells, swap(jnp.stack(ys), jnp.stack(xs), 2))


def conv_dot(x_ref, w_ref, bands, px, half, transposed):
    ny, nm = x_ref.shape[1] - 2, x_ref.shape[2]
    c = w_ref.shape[1]
    lo = half * c
    parts = [
        x_ref[px + a, b : b + ny, :, lo : lo + 3 * c].reshape(ny * nm, 3 * c)
        for a in range(3)
        for b in range(3)
    ]
    lhs = jnp.concatenate(parts, 1)
    if transposed:
        return lax.dot_general(lhs, bands[half], NT, preferred_element_type=F32)
    return jnp.dot(lhs, bands[half], preferred_element_type=F32)


def fill_bands(w_ref, bands, transposed):
    c = w_ref.shape[1]
    zero = jnp.zeros((c, c), BF)
    for half in range(2):
        for s in range(9):
            for k in range(3):
                for o in range(2):
                    tap = (k + half) - (o + 2 * half) + 1
                    good = 0 <= tap <= 2
                    rows = slice((3 * s + k) * c, (3 * s + k + 1) * c)
                    cols = slice(o * c, (o + 1) * c)
                    if transposed:
                        bands[half, cols, rows] = w_ref[26 - 3 * s - tap] if good else zero
                    else:
                        bands[half, rows, cols] = w_ref[3 * s + tap] if good else zero


def grads_kernel(x_ref, c_ref, w1_ref, w2_ref, gp_ref, g1_ref, g2_ref, bands, pre, gh, hid_t, gp_t, hid):
    ny, nm = x_ref.shape[1] - 2, x_ref.shape[2]
    nj = ny // 2
    c = w1_ref.shape[1]
    fill_bands(w1_ref, bands, False)
    for px in range(2):
        for half in range(2):
            pre[px, :, 2 * half * c : 2 * (half + 1) * c] = conv_dot(x_ref, w1_ref, bands, px, half, False)
    zero = jnp.zeros((c, c), BF)
    for px in range(2):
        for py in range(2):
            total = None
            for a, ci in PAIRS[px]:
                for b, dj in PAIRS[py]:
                    w = lambda t: w2_ref[9 * a + 3 * b + t]
                    left = jnp.concatenate([w(1), w(2), zero, zero], 0)
                    right = jnp.concatenate([zero, w(0), w(1), w(2)], 0)
                    rhs = jnp.concatenate([left, right], 1)
                    lhs = c_ref[ci, dj : dj + nj].reshape(nj * nm, 2 * c)
                    term = lax.dot_general(lhs, rhs, NT, preferred_element_type=F32)
                    total = term if total is None else total + term
            gh[px, :, py] = total.reshape(nj, nm, 4 * c)

    for px in range(2):
        def cells(j, _):
            for py in range(2):
                y = 2 * j + py
                v = pre[px, pl.ds(pl.multiple_of(y * nm, nm), nm), :]
                sigma = jax.nn.sigmoid(v)
                hid[px, py, j] = (v * sigma).astype(BF)
                gp_ref[px, y] = (gh[px, j, py] * (sigma * (1.0 + v * (1.0 - sigma)))).astype(BF)
            return _

        lax.fori_loop(0, nj, cells, 0)
    for px in range(2):
        gp_t[:, px * ny * nm : (px + 1) * ny * nm] = gp_ref[px].reshape(ny * nm, 4 * c).T
        for py in range(2):
            hid_t[px, py] = hid[px, py].reshape(nj * nm, 4 * c).T
    for a in range(3):
        px = 0 if a == 1 else 1
        ci = 1 if a == 0 else 0
        for b in range(3):
            py = 0 if b == 1 else 1
            dj = 1 if b == 0 else 0
            rhs = c_ref[ci, dj : dj + nj].reshape(nj * nm, 2 * c)
            r = jnp.dot(hid_t[px, py], rhs, preferred_element_type=F32)
            blk = lambda z, k: r[z * c : (z + 1) * c, k * c : (k + 1) * c]
            t = 9 * a + 3 * b
            g2_ref[t] = blk(1, 1).astype(BF)
            g2_ref[t + 1] = (blk(0, 0) + blk(2, 1)).astype(BF)
            g2_ref[t + 2] = (blk(1, 0) + blk(3, 1)).astype(BF)
    for a in range(3):
        for b in range(3):
            sums = [None, None, None]
            for half in range(2):
                rhs = jnp.concatenate(
                    [
                        x_ref[px + a, b : b + ny, :, half * c : (half + 3) * c].reshape(ny * nm, 3 * c)
                        for px in range(2)
                    ],
                    0,
                )
                r = jnp.dot(gp_t[2 * half * c : 2 * (half + 1) * c, :], rhs, preferred_element_type=F32)
                for o in range(2):
                    for k in range(3):
                        tap = (k + half) - (o + 2 * half) + 1
                        if 0 <= tap <= 2:
                            term = r[o * c : (o + 1) * c, k * c : (k + 1) * c]
                            sums[tap] = term if sums[tap] is None else sums[tap] + term
            for tap in range(3):
                g1_ref[9 * a + 3 * b + tap] = sums[tap].T.astype(BF)


def volume_kernel(x_ref, w_ref, out_ref, bands):
    ny, nm = x_ref.shape[1] - 2, x_ref.shape[2]
    c = w_ref.shape[1]
    fill_bands(w_ref, bands, True)
    for px in range(2):
        for half in range(2):
            r = conv_dot(x_ref, w_ref, bands, px, half, True)
            out_ref[px, :, :, 2 * half * c : 2 * (half + 1) * c] = r.reshape(ny, nm, 2 * c).astype(BF)


PARAMS = pltpu.CompilerParams(vmem_limit_bytes=48 * 1024 * 1024)


def plane_orders(gx, gy):
    gys = [("gy", 1 << k) for k in range(gy.bit_length() - 1)]
    gxs = [("gx", 1 << k) for k in range(gx.bit_length() - 1)]
    return (gys + gxs, gys[:1] + gxs + gys[1:])


def by_halves(grad, order, gx, gy):
    taps, c, _ = grad.shape
    bits = [("gx", 1 << k) for k in reversed(range(gx.bit_length() - 1))]
    bits += [("gy", 1 << k) for k in reversed(range(gy.bit_length() - 1))]
    share = c // (gx * gy)
    parts = grad.reshape((taps,) + (2,) * len(bits) + (share, c))
    n = len(bits)
    parts = parts.transpose(tuple(1 + bits.index(o) for o in order) + (0, n + 1, n + 2))
    return parts.reshape(gx * gy, taps * share, c)


def reduce_kernel(orders, dps, first_ref, second_ref, out1_ref, out2_ref, *scratch):
    steps = len(orders[0]) + len(dps)
    lands, sums = scratch[:steps], scratch[steps : 2 * steps - 1]
    send_sem, recv_sem = scratch[-2:]
    outs = (out1_ref, out2_ref)

    def side(axis, bit):
        at = lax.axis_index(axis)
        mine = (at // bit) % 2
        return mine, {axis: at + bit * (1 - 2 * mine)}

    barrier = pltpu.get_barrier_semaphore()
    for axis, bit in orders[0] + dps:
        pl.semaphore_signal(
            barrier, inc=1, device_id=side(axis, bit)[1], device_id_type=pl.DeviceIdType.MESH
        )
    pl.semaphore_wait(barrier, steps)

    held = [first_ref, second_ref]
    halving = len(orders[0])
    plans = [orders[0] + dps, orders[1] + dps[::-1]]
    for k in range(steps):
        copies = []
        for s in range(2):
            mine, partner = side(*plans[s][k])
            size = lands[k].shape[1]
            src = held[s].at[pl.ds((1 - mine) * size, size)] if k < halving else held[s]
            copy = pltpu.make_async_remote_copy(
                src_ref=src,
                dst_ref=lands[k].at[s],
                send_sem=send_sem.at[k, s],
                recv_sem=recv_sem.at[k, s],
                device_id=partner,
                device_id_type=pl.DeviceIdType.MESH,
            )
            copy.start()
            copies.append(copy)
        following = []
        for s in range(2):
            copies[s].wait()
            mine, _ = side(*plans[s][k])
            size = lands[k].shape[1]
            target = outs[s] if k == steps - 1 else sums[k].at[s]
            base = mine * size if k < halving else 0

            def add(i, _):
                total = held[s][base + i].astype(F32) + lands[k][s, i].astype(F32)
                target[i] = total.astype(target.dtype)
                return _

            lax.fori_loop(0, size, add, 0)
            following.append(target)
        held = following


def reduce_grads(first, second):
    gx, gy, dp = (lax.axis_size(a) for a in ("gx", "gy", "dp"))
    orders = plane_orders(gx, gy)
    dps = [("dp", 1 << k) for k in range(dp.bit_length() - 1)]
    taps, c, _ = first.shape
    share = c // (gx * gy)
    rows = taps * share
    sizes = [gx * gy >> (k + 1) for k in range(len(orders[0]))] + [1] * len(dps)
    out = jax.ShapeDtypeStruct((1, rows, c), F32)
    one, two = pl.pallas_call(
        functools.partial(reduce_kernel, orders, dps),
        out_shape=(out, out),
        in_specs=[VMEM] * 2,
        out_specs=(VMEM,) * 2,
        scratch_shapes=[pltpu.VMEM((2, n, rows, c), BF) for n in sizes]
        + [pltpu.VMEM((2, n, rows, c), BF) for n in sizes[:-1]]
        + [pltpu.SemaphoreType.DMA((len(sizes), 2)), pltpu.SemaphoreType.DMA((len(sizes), 2))],
        compiler_params=pltpu.CompilerParams(
            collective_id=0, has_side_effects=True, vmem_limit_bytes=48 * 1024 * 1024
        ),
    )(by_halves(first, orders[0], gx, gy), by_halves(second, orders[1], gx, gy))
    return one.reshape(taps, share, c), two.reshape(taps, share, c)


def local(volume, cotangent, w_first, w_second):
    _, nx, ny, nz, c = volume.shape
    nm, nj, lanes = nx // 2, ny // 2, nz * c
    split = volume.reshape(nm, 2, ny, lanes).transpose(1, 2, 0, 3)
    cells, grads = widened_both(split, cotangent.reshape(nm, nj, 2 * c).transpose(1, 0, 2))
    weight = jax.ShapeDtypeStruct((27, c, c), BF)
    grad_pre, first, second = pl.pallas_call(
        grads_kernel,
        out_shape=(jax.ShapeDtypeStruct((2, ny, nm, lanes), BF), weight, weight),
        in_specs=[VMEM] * 4,
        out_specs=(VMEM,) * 3,
        scratch_shapes=[
            pltpu.VMEM((2, 27 * c, 2 * c), BF),
            pltpu.VMEM((2, ny * nm, lanes), F32),
            pltpu.VMEM((2, nj, 2, nm, lanes), F32),
            pltpu.VMEM((2, 2, lanes, nj * nm), BF),
            pltpu.VMEM((lanes, 2 * ny * nm), BF),
            pltpu.VMEM((2, 2, nj, nm, lanes), BF),
        ],
        compiler_params=PARAMS,
    )(cells, grads, w_first, w_second)
    share = reduce_grads(first, second)
    out = pl.pallas_call(
        volume_kernel,
        out_shape=jax.ShapeDtypeStruct((2, ny, nm, lanes), BF),
        in_specs=[VMEM] * 2,
        out_specs=VMEM,
        scratch_shapes=[pltpu.VMEM((2, 2 * c, 27 * c), BF)],
        compiler_params=PARAMS,
    )(widened_again(grad_pre), w_first)
    grad_volume = out.transpose(2, 0, 1, 3).reshape(1, nx, ny, nz, c)
    return (grad_volume, share[0], share[1])


def solution(mesh):
    return jax.shard_map(
        local,
        mesh=mesh,
        in_specs=(P("dp", "gx", "gy", None, None), P("dp", "gx", "gy", None, None), P(), P()),
        out_specs=(
            P("dp", "gx", "gy", None, None),
            P(None, ("gx", "gy"), None),
            P(None, ("gx", "gy"), None),
        ),
        check_vma=False,
    )
```

```python
import functools

import jax
import jax.numpy as jnp
from jax import lax
from jax.experimental import pallas as pl
from jax.experimental.pallas import tpu as pltpu
from jax.sharding import PartitionSpec as P

BF = jnp.bfloat16
F32 = jnp.float32
VMEM = pl.BlockSpec(memory_space=pltpu.VMEM)
NT = (((1,), (1,)), ((), ()))
PAIRS = (((1, 0),), ((0, 1), (2, 0)))


TURNS = [(dx, dy) for dx in (1, -1, 0) for dy in (1, -1, 0)][:8]


def swap_kernel(ys_ref, xs_ref, land_ref, send_sem, recv_sem):
    gx, gy = lax.axis_size("gx"), lax.axis_size("gy")
    x, y = lax.axis_index("gx"), lax.axis_index("gy")
    partners = [{"gx": (x + dx + gx) % gx, "gy": (y + dy + gy) % gy} for dx, dy in TURNS]
    barrier = pltpu.get_barrier_semaphore()
    for partner in partners:
        pl.semaphore_signal(barrier, inc=1, device_id=partner, device_id_type=pl.DeviceIdType.MESH)
    pl.semaphore_wait(barrier, len(TURNS))
    copies = []
    for k, (dx, dy) in enumerate(TURNS):
        src = ys_ref.at[(1 + dy) // 2] if dx == 0 else xs_ref.at[(1 + dx) // 2]
        copy = pltpu.make_async_remote_copy(
            src_ref=src,
            dst_ref=land_ref.at[k],
            send_sem=send_sem.at[k],
            recv_sem=recv_sem.at[k],
            device_id=partners[k],
            device_id_type=pl.DeviceIdType.MESH,
        )
        copy.start()
        copies.append(copy)
    for copy in copies:
        copy.wait()


def swap(ys, xs, place):
    land = pl.pallas_call(
        swap_kernel,
        out_shape=jax.ShapeDtypeStruct((8,) + ys.shape[1:], BF),
        in_specs=[VMEM] * 2,
        out_specs=VMEM,
        scratch_shapes=[pltpu.SemaphoreType.DMA((8,)), pltpu.SemaphoreType.DMA((8,))],
        compiler_params=pltpu.CompilerParams(collective_id=place, has_side_effects=True),
    )(ys, xs)
    return masked(land)


def masked(land):
    out = {}
    x, y = lax.axis_index("gx"), lax.axis_index("gy")
    has_x = {0: True, 1: x > 0, -1: x < lax.axis_size("gx") - 1}
    has_y = {0: True, 1: y > 0, -1: y < lax.axis_size("gy") - 1}
    for k, (dx, dy) in enumerate(TURNS):
        good = jnp.logical_and(has_x[dx], has_y[dy])
        out[dx, dy] = jnp.where(good, land[k], jnp.zeros((), BF))
    return out


def padded(rows, count, lanes):
    return jnp.pad(rows, ((0, count - rows.shape[0]), (0, lanes - rows.shape[1])))


def edges(cells):
    _, ny, nm, lanes = cells.shape
    rows = -(-max(2 * nm, ny) // 16) * 16
    ys = [padded(cells[:, y].reshape(2 * nm, lanes), rows, lanes) for y in (0, ny - 1)]
    xs = [padded(row, rows, lanes) for row in (cells[0, :, 0], cells[1, :, nm - 1])]
    return ys, xs


def widened(cells, got):
    _, ny, nm, lanes = cells.shape
    layer = lambda dy: got[0, dy][: 2 * nm].reshape(2, 1, nm, lanes)
    cells = jnp.concatenate([layer(1), cells, layer(-1)], 1)

    def column(dx):
        parts = [got[dx, 1][ny - 1 : ny], got[dx, 0][:ny], got[dx, -1][:1]]
        return jnp.concatenate(parts, 0)[:, None]

    even, odd = cells[0], cells[1]
    before = jnp.concatenate([column(1), odd[:, :-1]], 1)
    after = jnp.concatenate([even[:, 1:], column(-1)], 1)
    return jnp.stack([before, even, odd, after])


def widened_both(cells, coarse):
    lanes = cells.shape[3]
    nj, ni, few = coarse.shape
    ys, xs = edges(cells)
    top = ys[0].shape[0]
    more = -(-max(nj, ni) // 16) * 16
    low = lambda rows: padded(rows, more, lanes)
    blank = jnp.zeros((more, lanes), BF)
    ys = jnp.stack([jnp.concatenate([ys[0], low(coarse[0])]), jnp.concatenate([ys[1], blank])])
    xs = jnp.stack([jnp.concatenate([xs[0], low(coarse[:, 0])]), jnp.concatenate([xs[1], blank])])
    got = swap(ys, xs, 1)
    tail = lambda dx, dy, n: got[dx, dy][top : top + n, :few]
    long = jnp.concatenate([coarse, tail(0, -1, ni)[None]], 0)
    column = jnp.concatenate([tail(-1, 0, nj), tail(-1, -1, 1)], 0)[:, None]
    following = jnp.concatenate([long[:, 1:], column], 1)
    return widened(cells, got), jnp.stack([long, following])


def conv_dot(x_ref, w_ref, bands, px, half, transposed):
    ny, nm = x_ref.shape[1] - 2, x_ref.shape[2]
    c = w_ref.shape[1]
    lo = half * c
    parts = [
        x_ref[px + a, b : b + ny, :, lo : lo + 3 * c].reshape(ny * nm, 3 * c)
        for a in range(3)
        for b in range(3)
    ]
    lhs = jnp.concatenate(parts, 1)
    if transposed:
        return lax.dot_general(lhs, bands[half], NT, preferred_element_type=F32)
    return jnp.dot(lhs, bands[half], preferred_element_type=F32)


def fill_bands(w_ref, bands, transposed):
    c = w_ref.shape[1]
    zero = jnp.zeros((c, c), BF)
    for half in range(2):
        for s in range(9):
            for k in range(3):
                for o in range(2):
                    tap = (k + half) - (o + 2 * half) + 1
                    good = 0 <= tap <= 2
                    rows = slice((3 * s + k) * c, (3 * s + k + 1) * c)
                    cols = slice(o * c, (o + 1) * c)
                    if transposed:
                        bands[half, cols, rows] = w_ref[26 - 3 * s - tap] if good else zero
                    else:
                        bands[half, rows, cols] = w_ref[3 * s + tap] if good else zero


def grads_kernel(x_ref, c_ref, w1_ref, w2_ref, gp_ref, g1_ref, g2_ref, bands, pre, gh, hid_t, gp_t, hid):
    ny, nm = x_ref.shape[1] - 2, x_ref.shape[2]
    nj = ny // 2
    c = w1_ref.shape[1]
    fill_bands(w1_ref, bands, False)
    for px in range(2):
        for half in range(2):
            pre[px, :, 2 * half * c : 2 * (half + 1) * c] = conv_dot(x_ref, w1_ref, bands, px, half, False)
    zero = jnp.zeros((c, c), BF)
    for px in range(2):
        for py in range(2):
            total = None
            for a, ci in PAIRS[px]:
                for b, dj in PAIRS[py]:
                    w = lambda t: w2_ref[9 * a + 3 * b + t]
                    left = jnp.concatenate([w(1), w(2), zero, zero], 0)
                    right = jnp.concatenate([zero, w(0), w(1), w(2)], 0)
                    rhs = jnp.concatenate([left, right], 1)
                    lhs = c_ref[ci, dj : dj + nj].reshape(nj * nm, 2 * c)
                    term = lax.dot_general(lhs, rhs, NT, preferred_element_type=F32)
                    total = term if total is None else total + term
            gh[px, :, py] = total.reshape(nj, nm, 4 * c)

    for px in range(2):
        def cells(j, _):
            for py in range(2):
                y = 2 * j + py
                v = pre[px, pl.ds(pl.multiple_of(y * nm, nm), nm), :]
                sigma = jax.nn.sigmoid(v)
                hid[px, py, j] = (v * sigma).astype(BF)
                gp_ref[px, y] = (gh[px, j, py] * (sigma * (1.0 + v * (1.0 - sigma)))).astype(BF)
            return _

        lax.fori_loop(0, nj, cells, 0)
    for px in range(2):
        gp_t[:, px * ny * nm : (px + 1) * ny * nm] = gp_ref[px].reshape(ny * nm, 4 * c).T
        for py in range(2):
            hid_t[px, py] = hid[px, py].reshape(nj * nm, 4 * c).T
    for a in range(3):
        px = 0 if a == 1 else 1
        ci = 1 if a == 0 else 0
        for b in range(3):
            py = 0 if b == 1 else 1
            dj = 1 if b == 0 else 0
            rhs = c_ref[ci, dj : dj + nj].reshape(nj * nm, 2 * c)
            r = jnp.dot(hid_t[px, py], rhs, preferred_element_type=F32)
            blk = lambda z, k: r[z * c : (z + 1) * c, k * c : (k + 1) * c]
            t = 9 * a + 3 * b
            g2_ref[t] = blk(1, 1).astype(BF)
            g2_ref[t + 1] = (blk(0, 0) + blk(2, 1)).astype(BF)
            g2_ref[t + 2] = (blk(1, 0) + blk(3, 1)).astype(BF)
    for a in range(3):
        for b in range(3):
            sums = [None, None, None]
            for half in range(2):
                rhs = jnp.concatenate(
                    [
                        x_ref[px + a, b : b + ny, :, half * c : (half + 3) * c].reshape(ny * nm, 3 * c)
                        for px in range(2)
                    ],
                    0,
                )
                r = jnp.dot(gp_t[2 * half * c : 2 * (half + 1) * c, :], rhs, preferred_element_type=F32)
                for o in range(2):
                    for k in range(3):
                        tap = (k + half) - (o + 2 * half) + 1
                        if 0 <= tap <= 2:
                            term = r[o * c : (o + 1) * c, k * c : (k + 1) * c]
                            sums[tap] = term if sums[tap] is None else sums[tap] + term
            for tap in range(3):
                g1_ref[9 * a + 3 * b + tap] = sums[tap].T.astype(BF)


def volume_kernel(x_ref, w_ref, out_ref, bands):
    ny, nm = x_ref.shape[1] - 2, x_ref.shape[2]
    c = w_ref.shape[1]
    fill_bands(w_ref, bands, True)
    for px in range(2):
        for half in range(2):
            r = conv_dot(x_ref, w_ref, bands, px, half, True)
            out_ref[px, :, :, 2 * half * c : 2 * (half + 1) * c] = r.reshape(ny, nm, 2 * c).astype(BF)


PARAMS = pltpu.CompilerParams(vmem_limit_bytes=48 * 1024 * 1024)


def plane_orders(gx, gy):
    gys = [("gy", 1 << k) for k in range(gy.bit_length() - 1)]
    gxs = [("gx", 1 << k) for k in range(gx.bit_length() - 1)]
    return (gys + gxs, gys[:1] + gxs + gys[1:])


def by_halves(grad, order, gx, gy):
    taps, c, _ = grad.shape
    bits = [("gx", 1 << k) for k in reversed(range(gx.bit_length() - 1))]
    bits += [("gy", 1 << k) for k in reversed(range(gy.bit_length() - 1))]
    share = c // (gx * gy)
    parts = grad.reshape((taps,) + (2,) * len(bits) + (share, c))
    n = len(bits)
    parts = parts.transpose(tuple(1 + bits.index(o) for o in order) + (0, n + 1, n + 2))
    return parts.reshape(gx * gy, taps * share, c)


def reduce_kernel(orders, dps, first_ref, second_ref, ys_ref, xs_ref, out1_ref, out2_ref, land_ref, *scratch):
    steps = len(orders[0]) + len(dps)
    lands, sums = scratch[:steps], scratch[steps : 2 * steps - 1]
    send_sem, recv_sem, edge_send, edge_recv = scratch[-4:]
    outs = (out1_ref, out2_ref)

    def side(axis, bit):
        at = lax.axis_index(axis)
        mine = (at // bit) % 2
        return mine, {axis: at + bit * (1 - 2 * mine)}

    barrier = pltpu.get_barrier_semaphore()
    for axis, bit in orders[0] + dps:
        pl.semaphore_signal(
            barrier, inc=1, device_id=side(axis, bit)[1], device_id_type=pl.DeviceIdType.MESH
        )
    gx, gy = lax.axis_size("gx"), lax.axis_size("gy")
    x, y = lax.axis_index("gx"), lax.axis_index("gy")
    partners = [{"gx": (x + dx + gx) % gx, "gy": (y + dy + gy) % gy} for dx, dy in TURNS]
    for partner in partners:
        pl.semaphore_signal(barrier, inc=1, device_id=partner, device_id_type=pl.DeviceIdType.MESH)
    pl.semaphore_wait(barrier, steps + len(TURNS))
    edge_copies = []
    for k, (dx, dy) in enumerate(TURNS):
        copy = pltpu.make_async_remote_copy(
            src_ref=ys_ref.at[(1 + dy) // 2] if dx == 0 else xs_ref.at[(1 + dx) // 2],
            dst_ref=land_ref.at[k],
            send_sem=edge_send.at[k],
            recv_sem=edge_recv.at[k],
            device_id=partners[k],
            device_id_type=pl.DeviceIdType.MESH,
        )
        copy.start()
        edge_copies.append(copy)

    held = [first_ref, second_ref]
    halving = len(orders[0])
    plans = [orders[0] + dps, orders[1] + dps[::-1]]
    for k in range(steps):
        copies = []
        for s in range(2):
            mine, partner = side(*plans[s][k])
            size = lands[k].shape[1]
            src = held[s].at[pl.ds((1 - mine) * size, size)] if k < halving else held[s]
            copy = pltpu.make_async_remote_copy(
                src_ref=src,
                dst_ref=lands[k].at[s],
                send_sem=send_sem.at[k, s],
                recv_sem=recv_sem.at[k, s],
                device_id=partner,
                device_id_type=pl.DeviceIdType.MESH,
            )
            copy.start()
            copies.append(copy)
        following = []
        for s in range(2):
            copies[s].wait()
            mine, _ = side(*plans[s][k])
            size = lands[k].shape[1]
            target = outs[s] if k == steps - 1 else sums[k].at[s]
            base = mine * size if k < halving else 0

            def add(i, _):
                total = held[s][base + i].astype(F32) + lands[k][s, i].astype(F32)
                target[i] = total.astype(target.dtype)
                return _

            lax.fori_loop(0, size, add, 0)
            following.append(target)
        held = following
    for copy in edge_copies:
        copy.wait()


def reduce_grads(first, second, ys, xs):
    gx, gy, dp = (lax.axis_size(a) for a in ("gx", "gy", "dp"))
    orders = plane_orders(gx, gy)
    dps = [("dp", 1 << k) for k in range(dp.bit_length() - 1)]
    taps, c, _ = first.shape
    share = c // (gx * gy)
    rows = taps * share
    sizes = [gx * gy >> (k + 1) for k in range(len(orders[0]))] + [1] * len(dps)
    out = jax.ShapeDtypeStruct((1, rows, c), F32)
    one, two, land = pl.pallas_call(
        functools.partial(reduce_kernel, orders, dps),
        out_shape=(out, out, jax.ShapeDtypeStruct((8,) + ys.shape[1:], BF)),
        in_specs=[VMEM] * 4,
        out_specs=(VMEM,) * 3,
        scratch_shapes=[pltpu.VMEM((2, n, rows, c), BF) for n in sizes]
        + [pltpu.VMEM((2, n, rows, c), BF) for n in sizes[:-1]]
        + [pltpu.SemaphoreType.DMA((len(sizes), 2)), pltpu.SemaphoreType.DMA((len(sizes), 2))]
        + [pltpu.SemaphoreType.DMA((8,)), pltpu.SemaphoreType.DMA((8,))],
        compiler_params=pltpu.CompilerParams(
            collective_id=0, has_side_effects=True, vmem_limit_bytes=48 * 1024 * 1024
        ),
    )(by_halves(first, orders[0], gx, gy), by_halves(second, orders[1], gx, gy), ys, xs)
    return one.reshape(taps, share, c), two.reshape(taps, share, c), masked(land)


def local(volume, cotangent, w_first, w_second):
    _, nx, ny, nz, c = volume.shape
    nm, nj, lanes = nx // 2, ny // 2, nz * c
    split = volume.reshape(nm, 2, ny, lanes).transpose(1, 2, 0, 3)
    cells, grads = widened_both(split, cotangent.reshape(nm, nj, 2 * c).transpose(1, 0, 2))
    weight = jax.ShapeDtypeStruct((27, c, c), BF)
    grad_pre, first, second = pl.pallas_call(
        grads_kernel,
        out_shape=(jax.ShapeDtypeStruct((2, ny, nm, lanes), BF), weight, weight),
        in_specs=[VMEM] * 4,
        out_specs=(VMEM,) * 3,
        scratch_shapes=[
            pltpu.VMEM((2, 27 * c, 2 * c), BF),
            pltpu.VMEM((2, ny * nm, lanes), F32),
            pltpu.VMEM((2, nj, 2, nm, lanes), F32),
            pltpu.VMEM((2, 2, lanes, nj * nm), BF),
            pltpu.VMEM((lanes, 2 * ny * nm), BF),
            pltpu.VMEM((2, 2, nj, nm, lanes), BF),
        ],
        compiler_params=PARAMS,
    )(cells, grads, w_first, w_second)
    ys, xs = edges(grad_pre)
    *share, got = reduce_grads(first, second, jnp.stack(ys), jnp.stack(xs))
    out = pl.pallas_call(
        volume_kernel,
        out_shape=jax.ShapeDtypeStruct((2, ny, nm, lanes), BF),
        in_specs=[VMEM] * 2,
        out_specs=VMEM,
        scratch_shapes=[pltpu.VMEM((2, 2 * c, 27 * c), BF)],
        compiler_params=PARAMS,
    )(widened(grad_pre, got), w_first)
    grad_volume = out.transpose(2, 0, 1, 3).reshape(1, nx, ny, nz, c)
    return (grad_volume, share[0], share[1])


def solution(mesh):
    return jax.shard_map(
        local,
        mesh=mesh,
        in_specs=(P("dp", "gx", "gy", None, None), P("dp", "gx", "gy", None, None), P(), P()),
        out_specs=(
            P("dp", "gx", "gy", None, None),
            P(None, ("gx", "gy"), None),
            P(None, ("gx", "gy"), None),
        ),
        check_vma=False,
    )
```
